32 devices in a mesh: node: 4 (over z), local: 8 (over y, x, core).
Axes of the slice: x: 2, y: 2, z: 4, core: 2. Of those that a mesh axis runs over, the one named last changes fastest.
Arguments:
- tokens: bfloat16 [4096, 3584], P(('node', 'local')), may hold values from -6 to 6
- group_ids: int32 [4096, 2], P(('node', 'local')), may hold values from 0 to 3, as said below
- local_ids: int32 [4096, 8], P(('node', 'local')), may hold values from 0 to 7, as said below
- router: bfloat16 [3584, 32], replicated, may hold values from -0.09375 to 0.09375
- w_gate: bfloat16 [32, 3584, 1024], P(('node', 'local')), may hold values from -0.09375 to 0.09375
- w_up: bfloat16 [32, 3584, 1024], P(('node', 'local')), may hold values from -0.09375 to 0.09375
- w_down: bfloat16 [32, 1024, 3584], P(('node', 'local')), may hold values from -0.1875 to 0.1875
Outputs:
- moe_out: bfloat16 [4096, 3584], P(('node', 'local'))
The draws below stay inside these ranges and needn't reach their ends.
Inputs may be any that keep to these rules, and one draw needn't show every extreme that they name: `group_ids`: each token names two different node groups; the tokens of one device name every node group exactly 64 times. `local_ids`: entry k names an expert of node group group_ids[t, k // 4]; the four entries of one group are different. The tokens of one device route at most 40 tokens to one expert, and in every node group some expert receives exactly 40 tokens from every device.
All inputs are finite; a program needn't handle non-finite values.
Results may differ from the reference program's by a relative error of at most 0.0058.
Values may be sent and summed in bfloat16 or wider, within the bound.
A program may use at most 128 MiB of HBM per device.

```python
import jax
import jax.numpy as jnp
from jax import lax

D = 3584
FF = 1024
TOK_DEV = 128
TOKENS = 4096
EXPERTS = 32
GROUP_EXP = 8
CAP = 40
N_NODE = 4
N_LOCAL = 8


def route_tables(key):
    base_key = jax.random.fold_in(key, 7)
    hot_expert = jax.random.randint(jax.random.fold_in(base_key, 1), (N_NODE,), 0, GROUP_EXP)
    pick_steps = jnp.arange(4, dtype=jnp.int32)
    node_range = jnp.arange(N_NODE, dtype=jnp.int32)

    def one_block(block_index):
        block_key = jax.random.fold_in(base_key, block_index + 2)
        key_rank, key_offset, key_shuffle = jax.random.split(block_key, 3)
        token_rank = jax.random.permutation(key_rank, TOK_DEV).astype(jnp.int32)
        first_group = token_rank % N_NODE
        second_group = (first_group + 1 + token_rank // N_NODE % (N_NODE - 1)) % N_NODE
        groups = jnp.stack([first_group, second_group], axis=1)
        member = ((first_group[:, None] == node_range[None, :]) | (second_group[:, None] == node_range[None, :])).astype(jnp.int32)
        by_rank = jnp.argsort(token_rank)
        sorted_member = member[by_rank]
        earlier = jnp.cumsum(sorted_member, axis=0) - sorted_member
        list_place = earlier[token_rank]
        position = jnp.take_along_axis(list_place, groups, axis=1)
        offset = jax.random.randint(key_offset, (N_NODE,), 0, GROUP_EXP - 1)
        hot_tok = hot_expert[groups]
        capped = jnp.minimum(position, CAP)
        start_at = 3 * capped + 4 * (position - capped) + offset[groups]
        has_hot = position < CAP
        step_shift = jnp.where(has_hot[:, :, None], pick_steps[None, None, :] - 1, pick_steps[None, None, :])
        cycle_index = (start_at[:, :, None] + step_shift) % (GROUP_EXP - 1)
        drawn_pick = cycle_index + (cycle_index >= hot_tok[:, :, None]).astype(jnp.int32)
        group_picks = jnp.where(has_hot[:, :, None] & (pick_steps == 0)[None, None, :], hot_tok[:, :, None], drawn_pick)
        scores = jax.random.randint(key_shuffle, (TOK_DEV, 2, 4), 0, 1 << 20) * 4 + pick_steps[None, None, :]
        shuffle = jnp.argsort(scores, axis=2)
        group_picks = jnp.take_along_axis(group_picks, shuffle, axis=2)
        return (groups, group_picks.reshape(TOK_DEV, 8))
    groups, local_picks = jax.vmap(one_block)(jnp.arange(TOKENS // TOK_DEV, dtype=jnp.int32))
    return (groups.reshape(TOKENS, 2).astype(jnp.int32), local_picks.reshape(TOKENS, 8).astype(jnp.int32))


def draw_group_ids(key, part):
    return route_tables(key)[0]


def draw_local_ids(key, part):
    return route_tables(key)[1]


def levels(own_key, extent, pieces, least, high):
    level = 1.0
    for dim, parts in pieces:
        steps = jax.random.uniform(jax.random.fold_in(jax.random.fold_in(own_key, 6), dim), (parts,), jnp.float32, least / len(pieces), high / len(pieces))
        level = level * jnp.repeat(jnp.exp(steps), extent[dim] // parts).reshape((-1,) + (1,) * (len(extent) - 1 - dim))
    return level


def scatter_about(stream_key, shape, spread, limit, cuts=(), kind=jnp.bfloat16):
    factor_of = levels(stream_key, shape, cuts, -0.22, 0.18) if cuts else 1.0
    array = jax.random.normal(stream_key, shape, jnp.float32) * spread * factor_of
    return jnp.minimum(jnp.maximum(array, -limit), limit).astype(kind)


def setup_inputs(seed: int = 0) -> dict:
    keys = jax.random.split(jax.random.key(seed), 8)
    return {
        "tokens": scatter_about(keys[0], (TOKENS, D), 1.0, 6.0, ((0, 32),)),
        "group_ids": draw_group_ids(jax.random.fold_in(keys[7], 71), 0),
        "local_ids": draw_local_ids(jax.random.fold_in(keys[7], 71), 0),
        "router": scatter_about(keys[3], (D, EXPERTS), D ** -0.5, 0.09375),
        "w_gate": scatter_about(keys[4], (EXPERTS, D, FF), D ** -0.5, 0.09375, ((0, 32),)),
        "w_up": scatter_about(keys[5], (EXPERTS, D, FF), D ** -0.5, 0.09375, ((0, 32),)),
        "w_down": scatter_about(keys[6], (EXPERTS, FF, D), FF ** -0.5, 0.1875, ((0, 32),)),
    }


def reference(tokens, group_ids, local_ids, router, w_gate, w_up, w_down):
    per_group = local_ids.shape[1] // group_ids.shape[1]
    picks_all = local_ids.shape[1]
    expert_ids = (jnp.repeat(group_ids, per_group, axis=1) * GROUP_EXP + local_ids).astype(jnp.int32)
    affinity = jax.nn.sigmoid(jnp.dot(tokens, router, preferred_element_type=jnp.float32))
    picked = jnp.take_along_axis(affinity, expert_ids, axis=1)
    weights = 2.5 * picked / jnp.sum(picked, axis=1, keepdims=True)
    flat_ids = expert_ids.reshape(-1)
    flat_weights = weights.reshape(-1)
    most_rows = N_NODE * N_LOCAL * CAP

    def visit_expert(running_sum, inputs):
        expert, gate_mat, up_mat, down_mat = inputs
        routed_mask = flat_ids == expert
        found_at = jnp.nonzero(routed_mask, size=most_rows, fill_value=0)[0].astype(jnp.int32)
        is_valid = jnp.arange(most_rows, dtype=jnp.int32) < jnp.sum(routed_mask.astype(jnp.int32))
        token_index = (found_at // picks_all).astype(jnp.int32)
        picked_rows = tokens[token_index]
        gate_part = jnp.dot(picked_rows, gate_mat, preferred_element_type=jnp.float32)
        up_part = jnp.dot(picked_rows, up_mat, preferred_element_type=jnp.float32)
        hidden = (jax.nn.silu(gate_part) * up_part).astype(jnp.bfloat16)
        expert_out = jnp.dot(hidden, down_mat, preferred_element_type=jnp.float32).astype(jnp.bfloat16)
        row_scale = jnp.where(is_valid, flat_weights[found_at], jnp.zeros((), flat_weights.dtype))
        running_sum = running_sum.at[token_index].add(row_scale[:, None] * expert_out.astype(running_sum.dtype))
        return running_sum, None

    start_sum = jnp.zeros((tokens.shape[0], tokens.shape[1]), jnp.float32)
    running_sum, _ = lax.scan(visit_expert, start_sum, (jnp.arange(EXPERTS, dtype=jnp.int32), w_gate, w_up, w_down))
    return running_sum.astype(jnp.bfloat16)
```

```python
import functools

import jax
import jax.numpy as jnp
from jax import lax
from jax.experimental import pallas as pl
from jax.experimental.pallas import tpu as pltpu
from jax.sharding import PartitionSpec as P

MESH = pl.DeviceIdType.MESH
META = 128
F32 = jnp.float32
BF16 = jnp.bfloat16


def slot_positions(targets, bins):
    onehot = (targets[:, None] == jnp.arange(bins, dtype=jnp.int32)[None, :]).astype(F32)
    count = targets.shape[0]
    before = jnp.tril(jnp.ones((count, count), F32), -1)
    earlier = jnp.dot(before, onehot, preferred_element_type=F32)
    return jnp.sum(earlier * onehot, axis=1).astype(jnp.int32)


def fill_slots(source_rows, owners, slot_index, slot_total):
    src_table = jnp.full((slot_total,), source_rows.shape[0], jnp.int32).at[slot_index].set(owners)
    padded = jnp.concatenate(
        [source_rows, jnp.zeros((1, source_rows.shape[1]), source_rows.dtype)], axis=0
    )
    return padded[src_table]


def expert_rows(flat_rows, w_gate, w_up, w_down):
    gate_part = jnp.dot(flat_rows, w_gate[0], preferred_element_type=F32)
    up_part = jnp.dot(flat_rows, w_up[0], preferred_element_type=F32)
    hidden = (jax.nn.silu(gate_part) * up_part).astype(BF16)
    return jnp.dot(hidden, w_down[0], preferred_element_type=F32).astype(BF16)


def on_device_general(tokens, group_ids, local_ids, router, w_gate, w_up, w_down):
    tok_dev, feat_width = tokens.shape
    node_size = lax.axis_size("node")
    local_size = lax.axis_size("local")
    cap_rows = 5 * tok_dev // (2 * local_size)
    group_count = group_ids.shape[1]
    per_group = local_ids.shape[1] // group_count
    expert_ids = jnp.repeat(group_ids, per_group, axis=1) * local_size + local_ids
    affinity = jax.nn.sigmoid(jnp.dot(tokens, router, preferred_element_type=F32))
    picked = jnp.take_along_axis(affinity, expert_ids, axis=1)
    picked_total = jnp.sum(picked, axis=1)
    node_rows = group_count * tok_dev // node_size
    flat_groups = group_ids.reshape(-1)
    home_slot = flat_groups * node_rows + slot_positions(flat_groups, node_size)
    home_owner = jnp.arange(flat_groups.shape[0], dtype=jnp.int32) // group_count
    outgoing = fill_slots(tokens, home_owner, home_slot, node_size * node_rows).reshape(
        node_size, node_rows, feat_width
    )
    outgoing_ids = (
        jnp.zeros((node_size * node_rows, per_group), jnp.int32)
        .at[home_slot]
        .set(local_ids.reshape(-1, per_group))
        .reshape(node_size, node_rows, per_group)
    )
    relay_in, relay_ids = (
        lax.all_to_all(outgoing, "node", split_axis=0, concat_axis=0, tiled=True),
        lax.all_to_all(outgoing_ids, "node", split_axis=0, concat_axis=0, tiled=True),
    )
    relay_flat = relay_in.reshape(-1, feat_width)
    relay_targets = relay_ids.reshape(-1)
    relay_cap = node_size * cap_rows
    relay_slot = relay_targets * relay_cap + slot_positions(relay_targets, local_size)
    relay_owner = jnp.arange(relay_targets.shape[0], dtype=jnp.int32) // per_group
    relay_send = fill_slots(relay_flat, relay_owner, relay_slot, local_size * relay_cap).reshape(
        local_size, relay_cap, feat_width
    )
    received = lax.all_to_all(relay_send, "local", split_axis=0, concat_axis=0, tiled=True)
    lead_size, item_count, _ = received.shape
    produced = expert_rows(received.reshape(-1, feat_width), w_gate, w_up, w_down).reshape(
        lead_size, item_count, feat_width
    )
    relay_back = lax.all_to_all(produced, "local", split_axis=0, concat_axis=0, tiled=True)
    relay_terms = relay_back.reshape(-1, feat_width)[relay_slot].reshape(-1, per_group, feat_width)
    relay_aff = jax.nn.sigmoid(jnp.dot(relay_flat, router, preferred_element_type=F32))
    relay_cols = lax.axis_index("node") * local_size + relay_ids.reshape(-1, per_group)
    relay_score = jnp.take_along_axis(relay_aff, relay_cols, axis=1)
    partial_sum = jnp.sum(relay_score[:, :, None] * relay_terms.astype(F32), axis=1)
    home_back = lax.all_to_all(
        partial_sum.reshape(node_size, node_rows, feat_width),
        "node",
        split_axis=0,
        concat_axis=0,
        tiled=True,
    )
    home_sum = jnp.sum(
        home_back.reshape(-1, feat_width)[home_slot].reshape(tok_dev, group_count, feat_width),
        axis=1,
    )
    mixed = (2.5 / picked_total)[:, None] * home_sum
    return mixed.astype(BF16)


OWN_X, OWN_Y, OWN_S, FWD_Y, FWD_X, SIB_X, SIB_Y, SIB_D, PART_S, DIAG_X, DIAG_Y, SUM_X, SUM_Y, HOME, NODE = range(15)


def layer_kernel(
    n, rows, d, ff,
    out_ref, wg_hbm, wu_hbm, wd_hbm,
    home, xh,
    wg, wu, wd, xv, hid, ysend, ykeep, sib, dg, rx, ry,
    ss, rs, wsem, xsem, csem,
):
    z = lax.axis_index("node")
    l = lax.axis_index("local")

    def flip(b):
        return l + b - 2 * b * ((l // b) % 2)

    sibling, xn, yn = (z, flip(1)), (z, flip(2)), (z, flip(4))
    half = rows // 2

    weights = [
        pltpu.make_async_copy(wg_hbm, wg, wsem.at[0]),
        pltpu.make_async_copy(wu_hbm, wu, wsem.at[1]),
        pltpu.make_async_copy(wd_hbm, wd, wsem.at[2]),
    ]
    first = pltpu.make_async_copy(out_ref.at[0], xh.at[0, 0, pl.ds(0, rows)], csem.at[0])
    first.start()

    barrier = pltpu.get_barrier_semaphore()
    peers = [sibling, xn, yn] + [(lax.rem(z + s, n), l) for s in range(1, n)]
    for peer in peers:
        pl.semaphore_signal(barrier, inc=1, device_id=peer, device_id_type=MESH)
    pl.semaphore_wait(barrier, len(peers))

    def copy(s, kind, src, dst, dev):
        return pltpu.make_async_remote_copy(
            src_ref=src, dst_ref=dst, send_sem=ss.at[s, kind], recv_sem=rs.at[s, kind],
            device_id=dev, device_id_type=MESH,
        )

    def blk(s, c, r, at=0, size=rows):
        return xh.at[s, c, pl.ds(r * rows + at, size)]

    def kp(s, r, at=0, size=rows):
        return ykeep.at[s % 2, pl.ds(r * rows + at, size)]

    cp = {}
    for s in range(n):
        cp[s, OWN_X] = copy(s, OWN_X, blk(s, 0, 0), blk(s, 0, 1), xn)
        cp[s, OWN_Y] = copy(s, OWN_Y, blk(s, 0, 0), blk(s, 0, 2), yn)
        cp[s, OWN_S] = copy(s, OWN_S, blk(s, 0, 0), blk(s, 1, 0), sibling)
        cp[s, FWD_Y] = copy(s, FWD_Y, blk(s, 0, 1, 0, half), blk(s, 0, 3, 0, half), yn)
        cp[s, FWD_X] = copy(s, FWD_X, blk(s, 0, 2, half, half), blk(s, 0, 3, half, half), xn)
        cp[s, SIB_X] = copy(s, SIB_X, blk(s, 0, 1), blk(s, 1, 1), sibling)
        cp[s, SIB_Y] = copy(s, SIB_Y, blk(s, 0, 2), blk(s, 1, 2), sibling)
        cp[s, SIB_D] = copy(s, SIB_D, blk(s, 0, 3), blk(s, 1, 3), sibling)
        cp[s, PART_S] = copy(s, PART_S, ysend.at[s % 2], sib.at[s], sibling)
        cp[s, DIAG_X] = copy(s, DIAG_X, kp(s, 3, 0, half), dg.at[s, pl.ds(0, half)], xn)
        cp[s, DIAG_Y] = copy(s, DIAG_Y, kp(s, 3, half, half), dg.at[s, pl.ds(half, half)], yn)
        cp[s, SUM_X] = copy(s, SUM_X, kp(s, 1), rx.at[s], xn)
        cp[s, SUM_Y] = copy(s, SUM_Y, kp(s, 2), ry.at[s], yn)
        if s:
            cp[s, HOME] = copy(s, HOME, kp(s, 0), home.at[s], (lax.rem(z + s, n), l))
            cp[s, NODE] = copy(s, NODE, out_ref.at[s], blk(s, 0, 0), (lax.rem(z - s + n, n), l))
    last = pltpu.make_async_copy(kp(0, 0), home.at[0], csem.at[1])
    sends = []

    def start(s, *kinds):
        for k in kinds:
            cp[s, k].start()
            if k not in (PART_S, DIAG_X, DIAG_Y, SUM_X, SUM_Y, HOME):
                sends.append((s, k))

    def arrived(s, *kinds):
        for k in kinds:
            cp[s, k].wait_recv()

    def sent(s, *kinds):
        for k in kinds:
            cp[s, k].wait_send()

    def gather_own(s):
        if s:
            arrived(s, NODE)
        else:
            first.wait()
        start(s, OWN_X, OWN_Y, OWN_S)

    def gather_forward(s):
        arrived(s, OWN_X)
        start(s, FWD_Y, SIB_X)
        arrived(s, OWN_Y)
        start(s, FWD_X, SIB_Y)

    def gather_diagonal(s):
        arrived(s, FWD_Y, FWD_X)
        start(s, SIB_D)

    def load(s):
        arrived(s, OWN_S, SIB_X, SIB_Y, SIB_D)
        for c in (1, 0):
            pltpu.make_async_copy(xh.at[s, c], xv.at[c], xsem.at[c]).start()

    def expert(s, c):
        pltpu.make_async_copy(xh.at[s, c], xv.at[c], xsem.at[c]).wait()
        if s == 0 and c == 1:
            weights[0].wait()
            weights[1].wait()
        target = ysend if c else ykeep

        @pl.loop(0, ff // 256)
        def _(i):
            cols = pl.ds(pl.multiple_of(i * 256, 256), 256)
            x = xv[c, :, :d]
            g = jnp.dot(x, wg[:, cols], preferred_element_type=F32)
            u = jnp.dot(x, wu[:, cols], preferred_element_type=F32)
            hid[:, cols] = (g / (1.0 + jnp.exp(-g)) * u).astype(BF16)

        if s == 0 and c == 1:
            weights[2].wait()
        meta = xv[c, :, d:].astype(F32)
        lane = lax.broadcasted_iota(jnp.int32, meta.shape, 1)
        mine = (lane == l) | (lane == l + 8)
        scale = jnp.sum(jnp.where(mine, meta, 0.0), axis=1, keepdims=True)
        if s >= 2:
            if c:
                sent(s - 2, PART_S)
            else:
                sent(s - 2, DIAG_X, DIAG_Y, SUM_X, SUM_Y)
                if s > 2:
                    sent(s - 2, HOME)
                else:
                    last.wait()

        @pl.loop(0, d // 512)
        def _(i):
            cols = pl.ds(pl.multiple_of(i * 512, 512), 512)
            y = jnp.dot(hid[...], wd[:, cols], preferred_element_type=F32)
            target[s % 2, :, cols] = (scale * y).astype(BF16)

        if c:
            start(s, PART_S)

    def add(s, r, others, at=0, size=rows):
        @pl.loop(0, size // 16)
        def _(i):
            off = pl.multiple_of(i * 16, 16)
            here = pl.ds(r * rows + at + off, 16)
            total = ykeep[s % 2, here, :].astype(F32)
            for ref, base in others:
                total += ref[s, pl.ds(base + off, 16), :].astype(F32)
            ykeep[s % 2, here, :] = total.astype(BF16)

    def reduce_diagonal(s):
        arrived(s, PART_S)
        add(s, 3, [(sib, 3 * rows)])
        start(s, DIAG_X, DIAG_Y)

    def reduce_sides(s):
        arrived(s, DIAG_Y)
        add(s, 1, [(sib, rows)], 0, half)
        add(s, 1, [(sib, rows + half), (dg, half)], half, half)
        start(s, SUM_X)
        arrived(s, DIAG_X)
        add(s, 2, [(sib, 2 * rows), (dg, 0)], 0, half)
        add(s, 2, [(sib, 2 * rows + half)], half, half)
        start(s, SUM_Y)

    def reduce_home(s):
        arrived(s, SUM_X, SUM_Y)
        add(s, 0, [(sib, 0), (rx, 0), (ry, 0)])
        if s:
            start(s, HOME)
        else:
            last.start()

    for s in range(1, n):
        start(s, NODE)
    for w in weights:
        w.start()

    gather_own(0)
    gather_forward(0)
    if n > 1:
        gather_own(1)
    gather_diagonal(0)
    load(0)
    for s in range(n):
        expert(s, 1)
        if s + 1 < n:
            gather_forward(s + 1)
        if s + 2 < n:
            gather_own(s + 2)
        if s:
            reduce_sides(s - 1)
        expert(s, 0)
        if s + 1 < n:
            gather_diagonal(s + 1)
        reduce_diagonal(s)
        if s + 1 < n:
            load(s + 1)
        if s:
            reduce_home(s - 1)
    reduce_sides(n - 1)
    reduce_home(n - 1)

    for s in range(1, n):
        arrived(s, HOME)
    for s, k in sends:
        sent(s, k)
    for s in range(max(0, n - 2), n):
        sent(s, PART_S, DIAG_X, DIAG_Y, SUM_X, SUM_Y)
        if s:
            sent(s, HOME)
        else:
            last.wait()


def on_device_fused(tokens, group_ids, local_ids, router, w_gate, w_up, w_down):
    tok_dev, d = tokens.shape
    ff = w_gate.shape[2]
    n = lax.axis_size("node")
    local_size = lax.axis_size("local")
    group_count = group_ids.shape[1]
    per_group = local_ids.shape[1] // group_count
    rows = group_count * tok_dev // n
    z = lax.axis_index("node")

    affinity = jax.nn.sigmoid(jnp.dot(tokens, router, preferred_element_type=F32))
    expert_ids = jnp.repeat(group_ids, per_group, axis=1) * local_size + local_ids
    experts = jnp.arange(router.shape[1], dtype=jnp.int32)
    picked = jnp.sum(
        jnp.where(expert_ids[:, :, None] == experts, affinity[:, None, :], 0.0), axis=2
    )
    gate = 2.5 * picked / jnp.sum(picked, axis=1, keepdims=True)
    lanes = jnp.arange(local_size, dtype=jnp.int32)
    spread = jnp.sum(
        jnp.where(
            local_ids.reshape(tok_dev, group_count, per_group)[..., None] == lanes,
            gate.reshape(tok_dev, group_count, per_group)[..., None],
            0.0,
        ),
        axis=2,
    )
    high = lax.reduce_precision(spread, 8, 7)
    low = spread - high
    meta = jnp.concatenate(
        [high, low, jnp.zeros((tok_dev, group_count, META - 2 * local_size), F32)], axis=2
    ).astype(BF16)

    slots = []
    total = group_count * tok_dev
    before = jnp.tril(jnp.ones((tok_dev, tok_dev), BF16), -1)
    named = jnp.sum(
        (group_ids[:, :, None] == jnp.arange(n, dtype=jnp.int32)).astype(jnp.int32), axis=1
    )
    earlier = jnp.dot(before, named.astype(BF16), preferred_element_type=F32).astype(jnp.int32)
    place = jnp.sum(
        jnp.where(group_ids[:, :, None] == jnp.arange(n, dtype=jnp.int32), earlier[:, None, :], 0),
        axis=2,
    )
    slots = (z - group_ids + n) % n * rows + place
    picks = [
        (slots[None, :, j] == jnp.arange(total, dtype=jnp.int32)[:, None]).astype(BF16)
        for j in range(group_count)
    ]
    body = jnp.dot(sum(picks), tokens, preferred_element_type=F32)
    tail = sum(
        jnp.dot(picks[j], meta[:, j], preferred_element_type=F32) for j in range(group_count)
    )
    outgoing = jnp.concatenate([body.astype(BF16), tail.astype(BF16)], axis=1)
    outgoing = outgoing.reshape(n, rows, d + META)

    wide = local_size // 2 * rows
    any_spec = pl.BlockSpec(memory_space=pl.ANY)
    home, _ = pl.pallas_call(
        functools.partial(layer_kernel, n, rows, d, ff),
        out_shape=(
            jax.ShapeDtypeStruct((n, rows, d), BF16),
            jax.ShapeDtypeStruct((n, 2, wide, d + META), BF16),
        ),
        in_specs=[any_spec] * 4,
        out_specs=(any_spec, any_spec),
        scratch_shapes=[
            pltpu.VMEM((d, ff), BF16),
            pltpu.VMEM((d, ff), BF16),
            pltpu.VMEM((ff, d), BF16),
            pltpu.VMEM((2, wide, d + META), BF16),
            pltpu.VMEM((wide, ff), BF16),
            pltpu.VMEM((2, wide, d), BF16),
            pltpu.VMEM((2, wide, d), BF16),
            pltpu.VMEM((n, wide, d), BF16),
            pltpu.VMEM((n, rows, d), BF16),
            pltpu.VMEM((n, rows, d), BF16),
            pltpu.VMEM((n, rows, d), BF16),
            pltpu.SemaphoreType.DMA((n, 15)),
            pltpu.SemaphoreType.DMA((n, 15)),
            pltpu.SemaphoreType.DMA((3,)),
            pltpu.SemaphoreType.DMA((2,)),
            pltpu.SemaphoreType.DMA((2,)),
        ],
        compiler_params=pltpu.CompilerParams(
            collective_id=0, has_side_effects=True, vmem_limit_bytes=60 * 2**20
        ),
        cost_estimate=pl.CostEstimate(
            flops=6 * n * 2 * wide * d * ff, bytes_accessed=40 * 2**20, transcendentals=0
        ),
    )(outgoing, w_gate[0], w_up[0], w_down[0])
    mixed = jnp.dot(sum(picks).T, home.reshape(total, d), preferred_element_type=F32)
    return mixed.astype(BF16)


def solution(mesh):
    fused = mesh.shape["local"] == 8
    return jax.shard_map(
        on_device_fused if fused else on_device_general,
        mesh=mesh,
        in_specs=(
            P(("node", "local"), None),
            P(("node", "local"), None),
            P(("node", "local"), None),
            P(),
            P(("node", "local"), None, None),
            P(("node", "local"), None, None),
            P(("node", "local"), None, None),
        ),
        out_specs=P(("node", "local"), None),
        check_vma=False,
    )
```

```python
import functools

import jax
import jax.numpy as jnp
from jax import lax
from jax.experimental import pallas as pl
from jax.experimental.pallas import tpu as pltpu
from jax.sharding import PartitionSpec as P

MESH = pl.DeviceIdType.MESH
META = 128
F32 = jnp.float32
BF16 = jnp.bfloat16


def slot_positions(targets, bins):
    onehot = (targets[:, None] == jnp.arange(bins, dtype=jnp.int32)[None, :]).astype(F32)
    count = targets.shape[0]
    before = jnp.tril(jnp.ones((count, count), F32), -1)
    earlier = jnp.dot(before, onehot, preferred_element_type=F32)
    return jnp.sum(earlier * onehot, axis=1).astype(jnp.int32)


def fill_slots(source_rows, owners, slot_index, slot_total):
    src_table = jnp.full((slot_total,), source_rows.shape[0], jnp.int32).at[slot_index].set(owners)
    padded = jnp.concatenate(
        [source_rows, jnp.zeros((1, source_rows.shape[1]), source_rows.dtype)], axis=0
    )
    return padded[src_table]


def expert_rows(flat_rows, w_gate, w_up, w_down):
    gate_part = jnp.dot(flat_rows, w_gate[0], preferred_element_type=F32)
    up_part = jnp.dot(flat_rows, w_up[0], preferred_element_type=F32)
    hidden = (jax.nn.silu(gate_part) * up_part).astype(BF16)
    return jnp.dot(hidden, w_down[0], preferred_element_type=F32).astype(BF16)


def on_device_general(tokens, group_ids, local_ids, router, w_gate, w_up, w_down):
    tok_dev, feat_width = tokens.shape
    node_size = lax.axis_size("node")
    local_size = lax.axis_size("local")
    cap_rows = 5 * tok_dev // (2 * local_size)
    group_count = group_ids.shape[1]
    per_group = local_ids.shape[1] // group_count
    expert_ids = jnp.repeat(group_ids, per_group, axis=1) * local_size + local_ids
    affinity = jax.nn.sigmoid(jnp.dot(tokens, router, preferred_element_type=F32))
    picked = jnp.take_along_axis(affinity, expert_ids, axis=1)
    picked_total = jnp.sum(picked, axis=1)
    node_rows = group_count * tok_dev // node_size
    flat_groups = group_ids.reshape(-1)
    home_slot = flat_groups * node_rows + slot_positions(flat_groups, node_size)
    home_owner = jnp.arange(flat_groups.shape[0], dtype=jnp.int32) // group_count
    outgoing = fill_slots(tokens, home_owner, home_slot, node_size * node_rows).reshape(
        node_size, node_rows, feat_width
    )
    outgoing_ids = (
        jnp.zeros((node_size * node_rows, per_group), jnp.int32)
        .at[home_slot]
        .set(local_ids.reshape(-1, per_group))
        .reshape(node_size, node_rows, per_group)
    )
    relay_in, relay_ids = (
        lax.all_to_all(outgoing, "node", split_axis=0, concat_axis=0, tiled=True),
        lax.all_to_all(outgoing_ids, "node", split_axis=0, concat_axis=0, tiled=True),
    )
    relay_flat = relay_in.reshape(-1, feat_width)
    relay_targets = relay_ids.reshape(-1)
    relay_cap = node_size * cap_rows
    relay_slot = relay_targets * relay_cap + slot_positions(relay_targets, local_size)
    relay_owner = jnp.arange(relay_targets.shape[0], dtype=jnp.int32) // per_group
    relay_send = fill_slots(relay_flat, relay_owner, relay_slot, local_size * relay_cap).reshape(
        local_size, relay_cap, feat_width
    )
    received = lax.all_to_all(relay_send, "local", split_axis=0, concat_axis=0, tiled=True)
    lead_size, item_count, _ = received.shape
    produced = expert_rows(received.reshape(-1, feat_width), w_gate, w_up, w_down).reshape(
        lead_size, item_count, feat_width
    )
    relay_back = lax.all_to_all(produced, "local", split_axis=0, concat_axis=0, tiled=True)
    relay_terms = relay_back.reshape(-1, feat_width)[relay_slot].reshape(-1, per_group, feat_width)
    relay_aff = jax.nn.sigmoid(jnp.dot(relay_flat, router, preferred_element_type=F32))
    relay_cols = lax.axis_index("node") * local_size + relay_ids.reshape(-1, per_group)
    relay_score = jnp.take_along_axis(relay_aff, relay_cols, axis=1)
    partial_sum = jnp.sum(relay_score[:, :, None] * relay_terms.astype(F32), axis=1)
    home_back = lax.all_to_all(
        partial_sum.reshape(node_size, node_rows, feat_width),
        "node",
        split_axis=0,
        concat_axis=0,
        tiled=True,
    )
    home_sum = jnp.sum(
        home_back.reshape(-1, feat_width)[home_slot].reshape(tok_dev, group_count, feat_width),
        axis=1,
    )
    mixed = (2.5 / picked_total)[:, None] * home_sum
    return mixed.astype(BF16)


OWN_X, OWN_Y, OWN_S, FWD_Y, FWD_X, SIB_X, SIB_Y, SIB_D, PART_S, DIAG_X, DIAG_Y, SUM_X, SUM_Y, HOME, NODE, EARLY_X, EARLY_Y = range(17)


def layer_kernel(
    n, rows, d, ff,
    out_ref, wg_hbm, wu_hbm, wd_hbm,
    home, xh,
    wg, wu, wd, xv, hid, ysend, ykeep, sib, dg, rx, ry,
    ss, rs, wsem, xsem, csem,
):
    z = lax.axis_index("node")
    l = lax.axis_index("local")

    def flip(b):
        return l + b - 2 * b * ((l // b) % 2)

    sibling, xn, yn = (z, flip(1)), (z, flip(2)), (z, flip(4))
    half = rows // 2

    weights = [
        pltpu.make_async_copy(wg_hbm, wg, wsem.at[0]),
        pltpu.make_async_copy(wu_hbm, wu, wsem.at[1]),
        pltpu.make_async_copy(wd_hbm, wd, wsem.at[2]),
    ]
    first = pltpu.make_async_copy(out_ref.at[0], xh.at[0, 0, pl.ds(0, rows)], csem.at[0])
    first.start()

    barrier = pltpu.get_barrier_semaphore()
    peers = [sibling, xn, yn] + [(lax.rem(z + s, n), l) for s in range(1, n)]
    for peer in peers:
        pl.semaphore_signal(barrier, inc=1, device_id=peer, device_id_type=MESH)
    pl.semaphore_wait(barrier, len(peers))

    def copy(s, kind, src, dst, dev):
        return pltpu.make_async_remote_copy(
            src_ref=src, dst_ref=dst, send_sem=ss.at[s, kind], recv_sem=rs.at[s, kind],
            device_id=dev, device_id_type=MESH,
        )

    def blk(s, c, r, at=0, size=rows):
        return xh.at[s, c, pl.ds(r * rows + at, size)]

    def kp(s, r, at=0, size=rows):
        return ykeep.at[s % 2, pl.ds(r * rows + at, size)]

    cp = {}
    for s in range(n):
        cp[s, OWN_X] = copy(s, OWN_X, blk(s, 0, 0), blk(s, 0, 1), xn)
        cp[s, OWN_Y] = copy(s, OWN_Y, blk(s, 0, 0), blk(s, 0, 2), yn)
        cp[s, OWN_S] = copy(s, OWN_S, blk(s, 0, 0), blk(s, 1, 0), sibling)
        cp[s, FWD_Y] = copy(s, FWD_Y, blk(s, 0, 1, 0, half), blk(s, 0, 3, 0, half), yn)
        cp[s, FWD_X] = copy(s, FWD_X, blk(s, 0, 2, half, half), blk(s, 0, 3, half, half), xn)
        cp[s, SIB_X] = copy(s, SIB_X, blk(s, 0, 1), blk(s, 1, 1), sibling)
        cp[s, SIB_Y] = copy(s, SIB_Y, blk(s, 0, 2), blk(s, 1, 2), sibling)
        cp[s, SIB_D] = copy(s, SIB_D, blk(s, 0, 3), blk(s, 1, 3), sibling)
        cp[s, PART_S] = copy(s, PART_S, ysend.at[s % 2], sib.at[s], sibling)
        cp[s, DIAG_X] = copy(s, DIAG_X, kp(s, 3, 0, half), dg.at[s, pl.ds(0, half)], xn)
        cp[s, DIAG_Y] = copy(s, DIAG_Y, kp(s, 3, half, half), dg.at[s, pl.ds(half, half)], yn)
        cp[s, SUM_X] = copy(s, SUM_X, kp(s, 1, half, half), rx.at[s, pl.ds(half, half)], xn)
        cp[s, EARLY_X] = copy(s, EARLY_X, kp(s, 1, 0, half), rx.at[s, pl.ds(0, half)], xn)
        cp[s, SUM_Y] = copy(s, SUM_Y, kp(s, 2, 0, half), ry.at[s, pl.ds(0, half)], yn)
        cp[s, EARLY_Y] = copy(s, EARLY_Y, kp(s, 2, half, half), ry.at[s, pl.ds(half, half)], yn)
        if s:
            cp[s, HOME] = copy(s, HOME, kp(s, 0), home.at[s], (lax.rem(z + s, n), l))
            cp[s, NODE] = copy(s, NODE, out_ref.at[s], blk(s, 0, 0), (lax.rem(z - s + n, n), l))
    last = pltpu.make_async_copy(kp(0, 0), home.at[0], csem.at[1])
    sends = []

    def start(s, *kinds):
        for k in kinds:
            cp[s, k].start()
            if k not in (PART_S, DIAG_X, DIAG_Y, SUM_X, SUM_Y, EARLY_X, EARLY_Y, HOME):
                sends.append((s, k))

    def arrived(s, *kinds):
        for k in kinds:
            cp[s, k].wait_recv()

    def sent(s, *kinds):
        for k in kinds:
            cp[s, k].wait_send()

    def gather_own(s):
        if s:
            arrived(s, NODE)
        else:
            first.wait()
        start(s, OWN_X, OWN_Y, OWN_S)

    def gather_forward(s):
        arrived(s, OWN_X)
        start(s, FWD_Y, SIB_X)
        arrived(s, OWN_Y)
        start(s, FWD_X, SIB_Y)

    def gather_diagonal(s):
        arrived(s, FWD_Y, FWD_X)
        start(s, SIB_D)

    def load(s):
        arrived(s, OWN_S, SIB_X, SIB_Y, SIB_D)
        for c in (1, 0):
            pltpu.make_async_copy(xh.at[s, c], xv.at[c], xsem.at[c]).start()

    def expert(s, c):
        pltpu.make_async_copy(xh.at[s, c], xv.at[c], xsem.at[c]).wait()
        if s == 0 and c == 1:
            weights[0].wait()
            weights[1].wait()
        target = ysend if c else ykeep

        @pl.loop(0, ff // 256)
        def _(i):
            cols = pl.ds(pl.multiple_of(i * 256, 256), 256)
            x = xv[c, :, :d]
            g = jnp.dot(x, wg[:, cols], preferred_element_type=F32)
            u = jnp.dot(x, wu[:, cols], preferred_element_type=F32)
            hid[:, cols] = (g / (1.0 + jnp.exp(-g)) * u).astype(BF16)

        if s == 0 and c == 1:
            weights[2].wait()
        meta = xv[c, :, d:].astype(F32)
        lane = lax.broadcasted_iota(jnp.int32, meta.shape, 1)
        mine = (lane == l) | (lane == l + 8)
        scale = jnp.sum(jnp.where(mine, meta, 0.0), axis=1, keepdims=True)
        if s >= 2:
            if c:
                sent(s - 2, PART_S)
            else:
                sent(s - 2, DIAG_X, DIAG_Y, SUM_X, SUM_Y, EARLY_X, EARLY_Y)
                if s > 2:
                    sent(s - 2, HOME)
                else:
                    last.wait()

        @pl.loop(0, d // 512)
        def _(i):
            cols = pl.ds(pl.multiple_of(i * 512, 512), 512)
            y = jnp.dot(hid[...], wd[:, cols], preferred_element_type=F32)
            target[s % 2, :, cols] = (scale * y).astype(BF16)

        if c:
            start(s, PART_S)

    def add(s, r, others, at=0, size=rows):
        @pl.loop(0, size // 16)
        def _(i):
            off = pl.multiple_of(i * 16, 16)
            here = pl.ds(r * rows + at + off, 16)
            total = ykeep[s % 2, here, :].astype(F32)
            for ref, base in others:
                total += ref[s, pl.ds(base + off, 16), :].astype(F32)
            ykeep[s % 2, here, :] = total.astype(BF16)

    def reduce_diagonal(s):
        arrived(s, PART_S)
        add(s, 3, [(sib, 3 * rows)])
        start(s, DIAG_X, DIAG_Y)
        add(s, 1, [(sib, rows)], 0, half)
        start(s, EARLY_X)
        add(s, 2, [(sib, 2 * rows + half)], half, half)
        start(s, EARLY_Y)

    def reduce_sides(s):
        arrived(s, DIAG_Y)
        add(s, 1, [(sib, rows + half), (dg, half)], half, half)
        start(s, SUM_X)
        arrived(s, DIAG_X)
        add(s, 2, [(sib, 2 * rows), (dg, 0)], 0, half)
        start(s, SUM_Y)

    def reduce_home(s):
        arrived(s, SUM_X, SUM_Y, EARLY_X, EARLY_Y)
        add(s, 0, [(sib, 0), (rx, 0), (ry, 0)])
        if s:
            start(s, HOME)
        else:
            last.start()

    for s in range(1, n):
        start(s, NODE)
    for w in weights:
        w.start()

    gather_own(0)
    gather_forward(0)
    if n > 1:
        gather_own(1)
    gather_diagonal(0)
    load(0)
    for s in range(n):
        expert(s, 1)
        if s + 1 < n:
            gather_forward(s + 1)
        if s == 0 and n > 2:
            gather_own(2)
        if s:
            reduce_sides(s - 1)
        expert(s, 0)
        if s + 1 < n:
            gather_diagonal(s + 1)
        reduce_diagonal(s)
        if s + 3 < n:
            gather_own(s + 3)
        if s + 1 < n:
            load(s + 1)
        if s:
            reduce_home(s - 1)
    reduce_sides(n - 1)
    reduce_home(n - 1)

    for s in range(1, n):
        arrived(s, HOME)
    for s, k in sends:
        sent(s, k)
    for s in range(max(0, n - 2), n):
        sent(s, PART_S, DIAG_X, DIAG_Y, SUM_X, SUM_Y, EARLY_X, EARLY_Y)
        if s:
            sent(s, HOME)
        else:
            last.wait()


def on_device_fused(tokens, group_ids, local_ids, router, w_gate, w_up, w_down):
    tok_dev, d = tokens.shape
    ff = w_gate.shape[2]
    n = lax.axis_size("node")
    local_size = lax.axis_size("local")
    group_count = group_ids.shape[1]
    per_group = local_ids.shape[1] // group_count
    rows = group_count * tok_dev // n
    z = lax.axis_index("node")

    affinity = jax.nn.sigmoid(jnp.dot(tokens, router, preferred_element_type=F32))
    expert_ids = jnp.repeat(group_ids, per_group, axis=1) * local_size + local_ids
    experts = jnp.arange(router.shape[1], dtype=jnp.int32)
    picked = jnp.sum(
        jnp.where(expert_ids[:, :, None] == experts, affinity[:, None, :], 0.0), axis=2
    )
    gate = 2.5 * picked / jnp.sum(picked, axis=1, keepdims=True)
    lanes = jnp.arange(local_size, dtype=jnp.int32)
    spread = jnp.sum(
        jnp.where(
            local_ids.reshape(tok_dev, group_count, per_group)[..., None] == lanes,
            gate.reshape(tok_dev, group_count, per_group)[..., None],
            0.0,
        ),
        axis=2,
    )
    high = lax.reduce_precision(spread, 8, 7)
    low = spread - high
    meta = jnp.concatenate(
        [high, low, jnp.zeros((tok_dev, group_count, META - 2 * local_size), F32)], axis=2
    ).astype(BF16)

    slots = []
    total = group_count * tok_dev
    before = jnp.tril(jnp.ones((tok_dev, tok_dev), BF16), -1)
    named = jnp.sum(
        (group_ids[:, :, None] == jnp.arange(n, dtype=jnp.int32)).astype(jnp.int32), axis=1
    )
    earlier = jnp.dot(before, named.astype(BF16), preferred_element_type=F32).astype(jnp.int32)
    place = jnp.sum(
        jnp.where(group_ids[:, :, None] == jnp.arange(n, dtype=jnp.int32), earlier[:, None, :], 0),
        axis=2,
    )
    slots = (z - group_ids + n) % n * rows + place
    picks = [
        (slots[None, :, j] == jnp.arange(total, dtype=jnp.int32)[:, None]).astype(BF16)
        for j in range(group_count)
    ]
    body = jnp.dot(sum(picks), tokens, preferred_element_type=F32)
    tail = sum(
        jnp.dot(picks[j], meta[:, j], preferred_element_type=F32) for j in range(group_count)
    )
    outgoing = jnp.concatenate([body.astype(BF16), tail.astype(BF16)], axis=1)
    outgoing = outgoing.reshape(n, rows, d + META)

    wide = local_size // 2 * rows
    any_spec = pl.BlockSpec(memory_space=pl.ANY)
    home, _ = pl.pallas_call(
        functools.partial(layer_kernel, n, rows, d, ff),
        out_shape=(
            jax.ShapeDtypeStruct((n, rows, d), BF16),
            jax.ShapeDtypeStruct((n, 2, wide, d + META), BF16),
        ),
        in_specs=[any_spec] * 4,
        out_specs=(any_spec, any_spec),
        scratch_shapes=[
            pltpu.VMEM((d, ff), BF16),
            pltpu.VMEM((d, ff), BF16),
            pltpu.VMEM((ff, d), BF16),
            pltpu.VMEM((2, wide, d + META), BF16),
            pltpu.VMEM((wide, ff), BF16),
            pltpu.VMEM((2, wide, d), BF16),
            pltpu.VMEM((2, wide, d), BF16),
            pltpu.VMEM((n, wide, d), BF16),
            pltpu.VMEM((n, rows, d), BF16),
            pltpu.VMEM((n, rows, d), BF16),
            pltpu.VMEM((n, rows, d), BF16),
            pltpu.SemaphoreType.DMA((n, 17)),
            pltpu.SemaphoreType.DMA((n, 17)),
            pltpu.SemaphoreType.DMA((3,)),
            pltpu.SemaphoreType.DMA((2,)),
            pltpu.SemaphoreType.DMA((2,)),
        ],
        compiler_params=pltpu.CompilerParams(
            collective_id=0, has_side_effects=True, vmem_limit_bytes=60 * 2**20
        ),
        cost_estimate=pl.CostEstimate(
            flops=6 * n * 2 * wide * d * ff, bytes_accessed=40 * 2**20, transcendentals=0
        ),
    )(outgoing, w_gate[0], w_up[0], w_down[0])
    mixed = jnp.dot(sum(picks).T, home.reshape(total, d), preferred_element_type=F32)
    return mixed.astype(BF16)


def solution(mesh):
    fused = mesh.shape["local"] == 8
    return jax.shard_map(
        on_device_fused if fused else on_device_general,
        mesh=mesh,
        in_specs=(
            P(("node", "local"), None),
            P(("node", "local"), None),
            P(("node", "local"), None),
            P(),
            P(("node", "local"), None, None),
            P(("node", "local"), None, None),
            P(("node", "local"), None, None),
        ),
        out_specs=P(("node", "local"), None),
        check_vma=False,
    )
```
